512 devices in a mesh: space: 32 (over z, y_hi), scen: 16 (over x, y_lo, core).
Axes of the slice: x: 4, y: 4 (y_hi: 2, y_lo: 2; y = y_hi * 2 + y_lo), z: 16, core: 2. Of those that a mesh axis runs over, the one named last changes fastest.
Arguments:
- start_fraction: bfloat16 [64, 24, 65536], P('scen', None, 'space'), may hold values from 0 to 1
- ore_value: bfloat16 [64, 24, 65536], P('scen', None, 'space'), may hold values from -6 to 6
- dual_price: float32 [64, 24, 65536], P('scen', None, 'space'), may hold values from -3 to 3
- patterns: bfloat16 [3, 512, 512], replicated, may hold values from -0.15625 to 0.15625
- cone_list: int32 [128, 3], P('space'), may hold values from 0 to 127, as said below
- node_list: int32 [2, 64], replicated, may hold values from 0 to 15, as said below
- probability: float32 [64], replicated, may hold values from 0.5 to 2
Outputs:
- fraction: float32 [64, 24, 65536], P('scen', None, 'space')
- dual_out: float32 [64, 24, 65536], P('scen', None, 'space')
The draws below stay inside these ranges and needn't reach their ends.
Inputs may be any that keep to these rules, and one draw needn't show every extreme that they name: `cone_list`: row i holds i, then tile i - 1 and tile i + 1 in an order drawn per tile; where a neighbour lies outside the slab the tile itself stands in its place. `node_list`: row 0 holds second-section nodes below 4, row 1 third-section nodes; every node holds a scenario, and scenarios that share a third-section node share their second-section node.
All inputs are finite; a program needn't handle non-finite values.
Results may differ from the reference program's by a relative error of at most 0.00079.
Values may be sent and summed in bfloat16 or wider, within the bound.
A program may use at most 64 MiB of HBM per device.

```python
import math
import jax
import jax.numpy as jnp
from jax import lax

TILE = 512
PERIODS = 24
SECTIONS = 4
NODES1 = 4
NODES2 = 16
ITERS = 2
PG_STEPS = 2
SCEN = 64
TILES = 128
BLOCKS = 65536


def draw_cone_list(key, part):
    tile_ids = jnp.arange(TILES, dtype=jnp.int32)
    flips = jax.random.randint(jax.random.fold_in(key, 11), (TILES,), 0, 2)
    left_tile = jnp.where(tile_ids == 0, tile_ids, tile_ids - 1)
    right_tile = jnp.where(tile_ids == TILES - 1, tile_ids, tile_ids + 1)
    first_slot = jnp.where(flips == 1, left_tile, right_tile)
    second_slot = jnp.where(flips == 1, right_tile, left_tile)
    return jnp.stack([tile_ids, first_slot, second_slot], axis=1).astype(jnp.int32)


def draw_node_list(key, part):
    order = jax.random.permutation(jax.random.fold_in(key, 21), SCEN).astype(jnp.int32)
    filler = jax.random.randint(jax.random.fold_in(key, 22), (SCEN,), 0, NODES2)
    second_nodes = jnp.where(order < NODES2, order, filler).astype(jnp.int32)
    parents = jax.random.permutation(jax.random.fold_in(key, 23), NODES1).astype(jnp.int32)
    parent_of = jnp.take(parents, jnp.arange(NODES2, dtype=jnp.int32) % NODES1)
    first_nodes = jnp.take(parent_of, second_nodes).astype(jnp.int32)
    return jnp.stack([first_nodes, second_nodes], axis=0).astype(jnp.int32)


def levels(stream_key, extent, cuts, least, top_value):
    loudness, own = 1.0, jax.random.fold_in(stream_key, 6)
    for axis_at, parts in cuts:
        steps = jnp.exp(jax.random.uniform(jax.random.fold_in(own, axis_at), (parts,), jnp.float32, least / len(cuts), top_value / len(cuts)))
        loudness = loudness * jnp.repeat(steps, extent[axis_at] // parts).reshape([-1 if axis == axis_at else 1 for axis in range(len(extent))])
    return loudness


def scatter_about(own_key, extent, deviation, limit, shards=(), kind=jnp.bfloat16):
    level = levels(own_key, extent, shards, -0.22, 0.18) if shards else 1.0
    drawn = jax.random.normal(own_key, extent, jnp.float32) * deviation * level
    return jnp.minimum(jnp.maximum(drawn, -limit), limit).astype(kind)


def setup_inputs(seed: int = 0) -> dict:
    key_list = jax.random.split(jax.random.key(seed), 8)
    start_fraction = jnp.clip(1.0 * jax.random.uniform(key_list[0], (SCEN, PERIODS, BLOCKS), jnp.float32) ** levels(key_list[0], (SCEN, PERIODS, BLOCKS), ((0, 16), (2, 32)), -0.2, 0.2), 0.0, 1.0).astype(jnp.bfloat16)
    ore_value = scatter_about(key_list[1], (SCEN, PERIODS, BLOCKS), 1.0, 6.0, ((0, 16), (2, 32)))
    dual_price = scatter_about(key_list[2], (SCEN, PERIODS, BLOCKS), 0.5, 3.0, ((0, 16), (2, 32)), jnp.float32)
    patterns = scatter_about(key_list[3], (3, TILE, TILE), (3 * TILE) ** -0.5, 0.15625)
    cone_list = draw_cone_list(jax.random.fold_in(key_list[7], 71), 0)
    node_list = draw_node_list(jax.random.fold_in(key_list[7], 71), 0)
    probability = jnp.clip(jnp.exp(jax.random.uniform(key_list[6], (SCEN,), jnp.float32, math.log(0.5), math.log(2.0))), 0.5, 2.0)
    return dict(start_fraction=start_fraction, ore_value=ore_value, dual_price=dual_price, patterns=patterns, cone_list=cone_list, node_list=node_list, probability=probability)


def node_weights(nodes, weights_in, count):
    return (nodes[:, None] == jnp.arange(count)[None, :]).astype(jnp.float32) * weights_in[:, None]


def upper_center(middle, node_list, probability, quarter):
    width_blocks = middle.shape[2]
    scen_count = middle.shape[0]
    root_sum = jnp.tensordot(probability, middle[:, :quarter], axes=1, precision=lax.Precision.HIGHEST)
    root_mean = root_sum / jnp.sum(probability)
    weight_one = node_weights(node_list[0], probability, NODES1)
    weight_two = node_weights(node_list[1], probability, NODES2)
    first_sum = jnp.tensordot(weight_one, middle[:, quarter:2 * quarter], axes=((0,), (0,)), precision=lax.Precision.HIGHEST)
    second_sum = jnp.tensordot(weight_two, middle[:, 2 * quarter:3 * quarter], axes=((0,), (0,)), precision=lax.Precision.HIGHEST)
    first_mean = first_sum / jnp.sum(weight_one, axis=0)[:, None, None]
    second_mean = second_sum / jnp.sum(weight_two, axis=0)[:, None, None]
    root_part = jnp.broadcast_to(root_mean[None], (scen_count, quarter, width_blocks))
    first_part = jnp.take(first_mean, node_list[0], axis=0)
    second_part = jnp.take(second_mean, node_list[1], axis=0)
    return jnp.concatenate([root_part, first_part, second_part], axis=1)


def tree_center(fraction, node_list, probability):
    quarter = fraction.shape[1] // SECTIONS
    upper = upper_center(fraction[:, :(SECTIONS - 1) * quarter], node_list, probability, quarter)
    return jnp.concatenate([upper, fraction[:, (SECTIONS - 1) * quarter:]], axis=1)


def descend(fraction, ore_value, dual_now, center, cone_list, patterns):
    rounded = fraction.astype(jnp.bfloat16)
    full_shape = fraction.shape
    tile_view = rounded.reshape(full_shape[0], full_shape[1], full_shape[2] // TILE, TILE)
    accumulated = jnp.zeros((fraction.size // TILE, TILE), jnp.float32)
    for cone_slot in range(3):
        picked = jnp.take(tile_view, cone_list[:, cone_slot], axis=2).reshape(-1, TILE)
        accumulated = accumulated + jnp.dot(picked, patterns[cone_slot], preferred_element_type=jnp.float32)
    cone_mix = accumulated.reshape(full_shape)
    gradient = -ore_value.astype(jnp.float32) + dual_now + 1.0 * (fraction - center) + 1.0 * (fraction - cone_mix)
    return jnp.clip(fraction - 0.4 * gradient, 0.0, 1.0)


def reference(start_fraction, ore_value, dual_price, patterns, cone_list, node_list, probability):
    fraction = start_fraction.astype(jnp.float32)
    dual_now = dual_price
    center = tree_center(fraction, node_list, probability)
    for ph_round in range(ITERS):
        for inner_step in range(PG_STEPS):
            fraction = descend(fraction, ore_value, dual_now, center, cone_list, patterns)
        center = tree_center(fraction, node_list, probability)
        dual_now = dual_now + 1.0 * (fraction - center)
    return fraction, dual_now
```

```python
import functools

import jax
import jax.numpy as jnp
from jax import lax
from jax.experimental import pallas as pl
from jax.experimental.pallas import tpu as pltpu
from jax.sharding import PartitionSpec as P

TILE = 512
ITERS = 2
F32 = jnp.float32
BF16 = jnp.bfloat16
MESH = pl.DeviceIdType.MESH

SCL = 4
PER = 24
ROWS = SCL * PER
TL = 4
CODE = 65534.0
LANES = 128
HALF = 32
MSG = 2 * HALF


def iota(shape, dim):
    return lax.broadcasted_iota(jnp.int32, shape, dim)


def div6(r):
    return (r * 43) >> 8


def div24(r):
    return (r * 171) >> 12


def split(x):
    hi = x.astype(BF16)
    return hi, (x - hi.astype(F32)).astype(BF16)


def encode(x):
    return jnp.round(x * CODE).astype(jnp.int32).astype(jnp.int16)


def decode(v):
    return split(v.astype(jnp.int32).astype(F32))


def dot(a, b):
    return jnp.dot(a, b, preferred_element_type=F32)


def dot_t(a, b):
    return lax.dot_general(a, b, (((1,), (1,)), ((), ())), preferred_element_type=F32)


def kernel(ns, nc, cone, start, ore, dual, pats_hbm, node_row, node_col, prob_row, f_out, d_out,
           rounded, halo, pats, ore_v, f, lin, dacc, cone_acc, sel, expand, weights,
           snd1, rcv1, snd2, rcv2,
           load_sem, out_sem, halo_send, halo_recv, s1_sem, r1_sem, s2_sem, r2_sem):
    sp = lax.axis_index("space")
    sc = lax.axis_index("scen")
    left = lax.rem(sp + ns - 1, ns)
    right = lax.rem(sp + 1, ns)

    def load(k, src, dst):
        return pltpu.make_async_copy(src, dst, load_sem.at[k])

    loads = []
    for t in range(TL):
        loads.append(load(t, start.at[:, pl.ds(t * TILE, TILE)], rounded.at[0, t]))
    loads.append(load(TL, pats_hbm, pats))
    for t in range(TL):
        loads.append(load(TL + 1 + t, dual.at[:, pl.ds(t * TILE, TILE)], dacc.at[t]))
    for t in range(TL):
        loads.append(load(2 * TL + 1 + t, ore.at[:, pl.ds(t * TILE, TILE)], ore_v.at[t]))
    for c in loads:
        c.start()

    barrier = pltpu.get_barrier_semaphore()
    for nb in (left, right):
        pl.semaphore_signal(barrier, inc=1, device_id=(nb, sc), device_id_type=MESH)

    @pl.loop(1, nc)
    def _(d):
        pl.semaphore_signal(barrier, inc=1, device_id=(sp, lax.rem(sc + d, nc)), device_id_type=MESH)

    prob = prob_row[...]
    pn = prob / jnp.sum(prob, axis=1, keepdims=True)
    lane = iota(pn.shape, 1)
    col = iota((MSG, ROWS), 1)
    row = iota((MSG, ROWS), 0)
    cs = div24(col)
    cp = col - PER * cs
    low = row >= HALF
    r = jnp.where(low, row - HALF, row)
    rs = div6(r)
    rq = r - 6 * rs
    section = jnp.where(low, 2, 1)
    picks = (rs < SCL) & (cs == rs) & (cp == 6 * section + rq)
    wcol = jnp.zeros((1, ROWS), F32)
    one_s = div24(iota((1, ROWS), 1))
    for s in range(SCL):
        ps = jnp.sum(jnp.where(lane == sc * SCL + s, pn, 0.0), axis=1, keepdims=True)
        wcol = jnp.where(one_s == s, ps, wcol)
    w_hi = wcol.astype(BF16).astype(F32)
    w_lo = wcol - w_hi
    w_half = jnp.where(low, w_lo, w_hi)
    once = jnp.where(picks, 1.0, jnp.where((rs == SCL) & (cp == rq), w_half, 0.0))
    sel[:, :ROWS] = once.astype(BF16)
    sel[:, ROWS:] = once.astype(BF16)

    er = iota((ROWS, MSG), 0)
    ec = iota((ROWS, MSG), 1)
    es = div24(er)
    ep = er - PER * es
    target = jnp.where(
        ep < 6, 24 + ep, jnp.where(ep < 12, es * 6 + ep - 6, HALF + es * 6 + ep - 12)
    )
    once = jnp.where((ec == target) & (ep < 18), 1.0, 0.0).astype(BF16)
    expand[:, :MSG] = once
    expand[:, MSG:] = once

    rounded[0, TL] = jnp.zeros((ROWS, TILE), BF16)
    row1 = iota((ROWS, 1), 0)
    upper = (row1 - PER * div24(row1)) < 18
    leaf = jnp.where(upper, 0.0, 1.0)
    half_up = jnp.where(upper, 0.5, 0.0)

    def start_halo(step):
        a = pltpu.make_async_remote_copy(
            rounded.at[step, 0], halo.at[step, 1], halo_send.at[step, 0], halo_recv.at[step, 1],
            device_id=(left, sc), device_id_type=MESH)
        b = pltpu.make_async_remote_copy(
            rounded.at[step, TL - 1], halo.at[step, 0], halo_send.at[step, 1], halo_recv.at[step, 0],
            device_id=(right, sc), device_id_type=MESH)
        a.start()
        b.start()
        return a, b

    def send_all(src, dst, s_sem, r_sem, k):
        @pl.loop(1, nc)
        def _(d):
            j = lax.rem(sc + d, nc)
            pltpu.make_async_remote_copy(
                src.at[k, j], dst.at[k, sc], s_sem.at[k], r_sem.at[k],
                device_id=(sp, j), device_id_type=MESH).start()

    def wait_all(buf, sem, k):
        part = buf.at[k, pl.ds(0, nc - 1)]
        pltpu.make_async_copy(part, part, sem.at[k]).wait()

    def pack(k, values):
        for t in range(TL):
            x = jnp.concatenate(split(values(t) - 0.5), axis=0)
            m = dot(sel[...], x)
            top = 4.0 * (m[24:32] + m[56:64])
            m = encode(jnp.concatenate([m[:24], top, m[32:]], axis=0))
            for q in range(TL):
                snd1[k, t * TL + q] = m[:, q * LANES:(q + 1) * LANES]

    def average(k):
        rcv1[k, sc] = snd1[k, sc]
        wait_all(rcv1, r1_sem, k)
        for h in range(2):
            hi, lo = decode(rcv1[k, :, h * HALF:(h + 1) * HALF, :].reshape(nc * HALF, LANES))
            y = dot(weights[h, 0], hi) + (dot(weights[h, 1], hi) + dot(weights[h, 0], lo))
            y = jnp.round(y).astype(jnp.int32).astype(jnp.int16)
            snd2[k, :, h * HALF:(h + 1) * HALF, :] = y.reshape(nc, HALF, LANES)
        send_all(snd2, rcv2, s2_sem, r2_sem, k)
        rcv2[k, sc] = snd2[k, sc]

    def slots(t):
        tile = sp * TL + t
        lid = jnp.maximum(tile - 1, 0)
        a = jnp.where(cone[t, 1] == lid, 1, 2)
        return a, 3 - a

    def cone_own(step):
        own = jnp.concatenate([rounded[step, t] for t in range(TL)], axis=0)
        cone_acc[...] = dot(own, pats[0])
        for k in (1, 2):
            picked = []
            for t in range(TL):
                a, b = slots(t)
                if t == 0:
                    picked.append(jnp.where(b == k, rounded[step, 1], jnp.zeros((), BF16)))
                elif t == TL - 1:
                    picked.append(jnp.where(a == k, rounded[step, TL - 2], jnp.zeros((), BF16)))
                else:
                    picked.append(rounded[step, jnp.where(a == k, t - 1, t + 1)])
            cone_acc[...] += dot(jnp.concatenate(picked, axis=0), pats[k])

    def cone_halo(step, copies):
        for c in copies:
            c.wait()
        a, _ = slots(0)
        lv = jnp.where(sp == 0, rounded[step, 0], halo[step, 0])
        cone_acc[:ROWS] += dot(lv, pats[a])
        _, b = slots(TL - 1)
        rv = jnp.where(sp == ns - 1, rounded[step, TL - 1], halo[step, 1])
        cone_acc[(TL - 1) * ROWS:] += dot(rv, pats[b])

    def chunks(body):
        for t in range(TL):
            for q in range(TILE // LANES):
                body(t, pl.ds(q * LANES, LANES), t * TL + q)

    def center_of(k, j, fv):
        hi, lo = decode(rcv2[k, j])
        c = dot(expand[...], jnp.concatenate([hi, lo], axis=0))
        return c * (1.0 / CODE) + half_up + leaf * fv

    def first_step(it, step):
        def body(t, ln, j):
            if it == 0:
                fv = rounded[0, t, :, ln].astype(F32)
                c = center_of(it, j, fv)
                g = dacc[t, :, ln] - ore_v[t, :, ln].astype(F32) - c
            else:
                fv = f[t, :, ln]
                c = center_of(it, j, fv)
                dv = dacc[t, :, ln] + (fv - c)
                dacc[t, :, ln] = dv
                g = dv - ore_v[t, :, ln].astype(F32) - c
            lin[t, :, ln] = g
            descend(t, ln, fv, g, step)
        chunks(body)

    def second_step(step):
        def body(t, ln, j):
            descend(t, ln, f[t, :, ln], lin[t, :, ln], step)
        chunks(body)

    def descend(t, ln, fv, g, step):
        grad = g + fv + (fv - cone_acc[t * ROWS:(t + 1) * ROWS, ln])
        fv = jnp.clip(fv - 0.4 * grad, 0.0, 1.0)
        f[t, :, ln] = fv
        if step < 3:
            rounded[step + 1, t, :, ln] = fv.astype(BF16)

    for c in loads[:TL]:
        c.wait()
    pack(0, lambda t: rounded[0, t].astype(F32))
    pl.semaphore_wait(barrier, nc + 1)
    send_all(snd1, rcv1, s1_sem, r1_sem, 0)
    copies = start_halo(0)

    n = nc * HALF
    s_of = iota((n, LANES), 0)
    dev, rr = s_of >> 5, s_of & 31
    s6 = div6(rr)
    c = iota((n, LANES), 1)
    for h in range(2):
        same = node_col[:, h:h + 1] == node_row[h:h + 1, :]
        raw = jnp.where(same, prob, 0.0)
        m = raw / jnp.sum(raw, axis=1, keepdims=True)
        m = jnp.concatenate([m, jnp.zeros((64, 64), F32)], axis=1)
        tail = jnp.where((iota((64, LANES), 0) == 0) & (iota((64, LANES), 1) == 64), 0.25, 0.0)
        m = jnp.concatenate([m, tail], axis=0)
        onehot = (s6 < SCL) & (c == dev * SCL + s6)
        if h == 0:
            onehot = onehot | ((s6 == SCL) & (c == 64))
        place = onehot.astype(F32).astype(BF16)
        q_row = iota((1, n), 1) & 31
        q_row = q_row - 6 * div6(q_row)
        for part, mp in enumerate(split(m)):
            for b in range(n // LANES):
                rows = slice(b * LANES, (b + 1) * LANES)
                moved = dot(place[rows], mp).astype(BF16)
                full = dot_t(moved, place)
                q_col = iota((LANES, 1), 0) & 31
                q_col = q_col - 6 * div6(q_col)
                weights[h, part, rows, :] = jnp.where(q_col == q_row, full, 0.0).astype(BF16)

    average(0)
    for c in loads[TL:]:
        c.wait()
    for it in range(ITERS):
        a, b = 2 * it, 2 * it + 1
        cone_own(a)
        cone_halo(a, copies)
        wait_all(rcv2, r2_sem, it)
        first_step(it, a)
        copies = start_halo(b)
        cone_own(b)
        cone_halo(b, copies)
        second_step(b)
        pack(it + 1, lambda t: f[t])
        send_all(snd1, rcv1, s1_sem, r1_sem, it + 1)
        if it + 1 < ITERS:
            copies = start_halo(b + 1)
        average(it + 1)

    outs = []
    for t in range(TL):
        o = pltpu.make_async_copy(f.at[t], f_out.at[:, pl.ds(t * TILE, TILE)], out_sem.at[t])
        o.start()
        outs.append(o)
    wait_all(rcv2, r2_sem, ITERS)

    def finish(t, ln, j):
        lin[t, :, ln] = dacc[t, :, ln] + (f[t, :, ln] - center_of(ITERS, j, f[t, :, ln]))
    for t in range(TL):
        for q in range(TILE // LANES):
            finish(t, pl.ds(q * LANES, LANES), t * TL + q)
        o = pltpu.make_async_copy(lin.at[t], d_out.at[:, pl.ds(t * TILE, TILE)], out_sem.at[TL + t])
        o.start()
        outs.append(o)
    for o in outs:
        o.wait()
    for k in range(ITERS + 1):
        wait_all(snd1, s1_sem, k)
        wait_all(snd2, s2_sem, k)


def body(start_fraction, ore_value, dual_price, patterns, cone_list, node_list, probability):
    ns, nc = lax.axis_size("space"), lax.axis_size("scen")
    blocks = start_fraction.shape[2]
    flat = (ROWS, blocks)
    anyspec = pl.BlockSpec(memory_space=pl.ANY)
    vspec = pl.BlockSpec(memory_space=pltpu.VMEM)
    sspec = pl.BlockSpec(memory_space=pltpu.SMEM)
    steps, avgs = 2 * ITERS, ITERS + 1
    dma = pltpu.SemaphoreType.DMA
    f, d = pl.pallas_call(
        functools.partial(kernel, ns, nc),
        out_shape=[jax.ShapeDtypeStruct(flat, F32)] * 2,
        in_specs=[sspec] + [anyspec] * 4 + [vspec] * 3,
        out_specs=[anyspec] * 2,
        scratch_shapes=[
            pltpu.VMEM((steps, TL + 1, ROWS, TILE), BF16),
            pltpu.VMEM((steps, 2, ROWS, TILE), BF16),
            pltpu.VMEM((3, TILE, TILE), BF16),
            pltpu.VMEM((TL, ROWS, TILE), BF16),
            pltpu.VMEM((TL, ROWS, TILE), F32),
            pltpu.VMEM((TL, ROWS, TILE), F32),
            pltpu.VMEM((TL, ROWS, TILE), F32),
            pltpu.VMEM((TL * ROWS, TILE), F32),
            pltpu.VMEM((MSG, 2 * ROWS), BF16),
            pltpu.VMEM((ROWS, 2 * MSG), BF16),
            pltpu.VMEM((2, 2, nc * HALF, nc * HALF), BF16),
            pltpu.VMEM((avgs, nc, MSG, LANES), jnp.int16),
            pltpu.VMEM((avgs, nc, MSG, LANES), jnp.int16),
            pltpu.VMEM((avgs, nc, MSG, LANES), jnp.int16),
            pltpu.VMEM((avgs, nc, MSG, LANES), jnp.int16),
            dma((3 * TL + 1,)),
            dma((2 * TL,)),
            dma((steps, 2)),
            dma((steps, 2)),
            dma((avgs,)),
            dma((avgs,)),
            dma((avgs,)),
            dma((avgs,)),
        ],
        compiler_params=pltpu.CompilerParams(
            collective_id=0, has_side_effects=True, vmem_limit_bytes=50 * 2**20
        ),
    )(
        cone_list,
        start_fraction.reshape(flat),
        ore_value.reshape(flat),
        dual_price.reshape(flat),
        patterns,
        node_list,
        node_list.T,
        probability.reshape(1, -1),
    )
    return f.reshape(start_fraction.shape), d.reshape(start_fraction.shape)


def solution(mesh):
    in_specs = (
        P("scen", None, "space"),
        P("scen", None, "space"),
        P("scen", None, "space"),
        P(),
        P("space", None),
        P(),
        P(),
    )
    out_specs = (P("scen", None, "space"), P("scen", None, "space"))
    return jax.shard_map(body, mesh=mesh, in_specs=in_specs, out_specs=out_specs, check_vma=False)
```

```python
import functools

import jax
import jax.numpy as jnp
from jax import lax
from jax.experimental import pallas as pl
from jax.experimental.pallas import tpu as pltpu
from jax.sharding import PartitionSpec as P

TILE = 512
STEPS = 4
F32 = jnp.float32
BF16 = jnp.bfloat16
I16 = jnp.int16
MESH = pl.DeviceIdType.MESH

SCEN = 64
SCL = 4
PER = 24
HOME = SCL * PER
TL = 4
SEC = 6
UNIT = SCL * SEC
HALF = TILE // 2
MSG = (2 * UNIT, HALF)
ROWS = SCEN * SEC
NCH = 2
CH = ROWS // NCH
SUB = 96
LIN_CODE = 32767.0 / 9.0
FRAC_CODE = 65534.0
GAIN_CODE = 32767.0 / 2.0


def iota(shape, dim):
    return lax.broadcasted_iota(jnp.int32, shape, dim)


def div(r, by, most):
    mul = (1 << 16) // by + 1
    assert all((v * mul) >> 16 == v // by for v in range(most))
    return (r * mul) >> 16


def split(x):
    hi = x.astype(BF16)
    return hi, (x - hi.astype(F32)).astype(BF16)


def to16(x):
    return jnp.round(x).astype(jnp.int32).astype(I16)


def from16(v):
    return v.astype(jnp.int32).astype(F32)


def dot(a, b):
    return jnp.dot(a, b, preferred_element_type=F32)


def dot_t(a, b):
    return lax.dot_general(a, b, (((1,), (1,)), ((), ())), preferred_element_type=F32)


def fold(x):
    return jnp.concatenate([x[:, :HALF], x[:, HALF:]], axis=0)


def kernel(ns, nc, cone_in, node_in, prob_in, start, ore, dual, pats_in, f_out, d_out,
           cone, node, prob_v, f0_v, ore_v, dual_v, pats, perm, back, mean,
           rounded, halo, f, low, lin, gain, cone_acc,
           snd_f, rcv_f, snd_l, rcv_l, snd_o, rcv_o, snd_d, rcv_d, out_f, out_d,
           load_sem, out_sem, halo_send, halo_recv, a_send, a_recv, b_send):
    sp = lax.axis_index("space")
    sc = lax.axis_index("scen")
    x = lax.div(sc, TL)
    t_own = lax.rem(sc, TL)
    first = t_own == 0
    last = t_own == TL - 1
    left = (jnp.where(first, lax.rem(sp + ns - 1, ns), sp), jnp.where(first, sc + TL - 1, sc - 1))
    right = (jnp.where(last, lax.rem(sp + 1, ns), sp), jnp.where(last, sc - (TL - 1), sc + 1))

    barrier = pltpu.get_barrier_semaphore()
    for nb in (left, right):
        pl.semaphore_signal(barrier, inc=1, device_id=nb, device_id_type=MESH)

    @pl.loop(1, nc)
    def _(d):
        pl.semaphore_signal(barrier, inc=1, device_id=(sp, lax.rem(sc + d, nc)), device_id_type=MESH)

    def load(k, src, dst):
        c = pltpu.make_async_copy(src, dst, load_sem.at[k])
        c.start()
        return c

    load_f0 = load(0, start, f0_v)
    load_ore = load(1, ore, ore_v)
    load_dual = load(2, dual, dual_v)
    load_node = load(3, node_in, node)
    load_prob = load(4, prob_in, prob_v)
    load_cone = load(5, cone_in, cone)
    load_pats = load(6, pats_in, pats)

    def places(shape, home_dim):
        h, g = iota(shape, home_dim), iota(shape, 1 - home_dim)
        hs = div(h, PER, HOME)
        hp = h - PER * hs
        hx = div(hp, SEC, PER)
        return (hx * UNIT + hs * SEC + (hp - SEC * hx)) == g

    perm[...] = jnp.where(places((HOME, HOME), 1), 1.0, 0.0).astype(BF16)
    back[...] = jnp.where(places((HOME, HOME), 0), 1.0, 0.0).astype(BF16)

    def send_all(src, dst, k):
        @pl.loop(1, nc)
        def _(d):
            j = lax.rem(sc + d, nc)
            pltpu.make_async_remote_copy(
                src.at[j], dst.at[sc], a_send.at[k], a_recv.at[k],
                device_id=(sp, j), device_id_type=MESH).start()

    def wait_all(buf, sem, k):
        part = buf.at[pl.ds(0, nc - 1)]
        pltpu.make_async_copy(part, part, sem.at[k]).wait()

    load_f0.wait()
    for t in range(TL):
        m = dot(perm[...], f0_v[:, t * TILE:(t + 1) * TILE])
        for g in range(nc // TL):
            snd_f[g * TL + t] = fold(m[g * UNIT:(g + 1) * UNIT]).astype(BF16)
    pl.semaphore_wait(barrier, nc + 1)
    send_all(snd_f, rcv_f, 0)
    rcv_f[sc] = snd_f[sc]

    load_ore.wait()
    load_dual.wait()
    for t in range(TL):
        ln = slice(t * TILE, (t + 1) * TILE)
        v = jnp.round((dual_v[:, ln] - ore_v[:, ln].astype(F32)) * LIN_CODE)
        hi, lo = split(v)
        m = dot(perm[...], hi) + dot(perm[...], lo)
        for g in range(nc // TL):
            snd_l[g * TL + t] = to16(fold(m[g * UNIT:(g + 1) * UNIT]))
    send_all(snd_l, rcv_l, 1)
    rcv_l[sc] = snd_l[sc]

    load_node.wait()
    load_prob.wait()
    prob = prob_v[...]
    nodes = jnp.where(x == 2, node[1:2, :], node[0:1, :])
    onehot = jnp.where(iota((16, SCEN), 0) == nodes, 1.0, 0.0)
    same = lax.dot_general(onehot.T.astype(BF16), onehot.astype(BF16), (((1,), (0,)), ((), ())),
                           preferred_element_type=F32)
    eye = jnp.where(iota((SCEN, SCEN), 0) == iota((SCEN, SCEN), 1), 1.0, 0.0)
    same = jnp.where(x == 0, jnp.ones_like(same), jnp.where(x == 3, eye, same))
    raw = same * prob
    m = raw / jnp.sum(raw, axis=1, keepdims=True)
    r = iota((ROWS, SCEN), 0)
    of = jnp.where(div(r, SEC, ROWS) == iota((ROWS, SCEN), 1), 1.0, 0.0).astype(BF16)
    rc = iota((ROWS, 1), 0)
    rr = iota((1, ROWS), 1)
    p_col = rc - SEC * div(rc, SEC, ROWS)
    p_row = rr - SEC * div(rr, SEC, ROWS)
    for k, part in enumerate(split(m)):
        moved = dot(of, part).astype(BF16)
        for b in range(ROWS // SUB):
            rows = slice(b * SUB, (b + 1) * SUB)
            full = dot_t(moved[rows], of)
            mean[k, rows, :] = jnp.where(p_col[rows] == p_row, full, 0.0).astype(BF16)

    def pieces(rows0, rows1):
        for r0 in range(rows0, rows1, SUB):
            for q in range(TILE // 128):
                yield slice(r0, r0 + SUB), slice(q * 128, (q + 1) * 128)

    def start_halo(step, c):
        rows = pl.ds(c * CH, CH)
        for side, nb in ((1, left), (0, right)):
            pltpu.make_async_remote_copy(
                rounded.at[step, rows], halo.at[step, side, rows],
                halo_send.at[step, side], halo_recv.at[step, side, c],
                device_id=nb, device_id_type=MESH).start()

    def wait_halo(step, c):
        for side in (0, 1):
            part = halo.at[step, side, pl.ds(c * CH, CH)]
            pltpu.make_async_copy(part, part, halo_recv.at[step, side, c]).wait()

    wait_all(rcv_f, a_recv, 0)
    for i in range(nc):
        v = rcv_f[i].astype(F32)
        rows = slice(i * UNIT, (i + 1) * UNIT)
        f[rows, :HALF] = v[:UNIT]
        f[rows, HALF:] = v[UNIT:]
    for c in range(NCH):
        for rows, ln in pieces(c * CH, (c + 1) * CH):
            rounded[0, rows, ln] = f[rows, ln].astype(BF16)
        start_halo(0, c)

    load_cone.wait()
    load_pats.wait()
    tile = sp * TL + t_own
    slot = jnp.where(cone[t_own, 1] == jnp.maximum(tile - 1, 0), 1, 2)
    at_left = tile == 0
    at_right = tile == ns * TL - 1

    def average(step):
        hi = rounded[step]
        c = dot(mean[0], hi) + dot(mean[1], hi)
        return c if step == 0 else c + dot(mean[0], low[...])

    cen = average(0)
    gain[...] = cen
    cone_acc[...] = dot(rounded[0], pats[0])
    wait_all(rcv_l, a_recv, 1)
    for i in range(nc):
        v = from16(rcv_l[i]) * (1.0 / LIN_CODE)
        rows = slice(i * UNIT, (i + 1) * UNIT)
        lin[rows, :HALF] = v[:UNIT] - gain[rows, :HALF]
        lin[rows, HALF:] = v[UNIT:] - gain[rows, HALF:]

    def step(s):
        for c in range(NCH):
            wait_halo(s, c)
            rc = slice(c * CH, (c + 1) * CH)
            lv = jnp.where(at_left, rounded[s, rc], halo[s, 0, rc])
            rv = jnp.where(at_right, rounded[s, rc], halo[s, 1, rc])
            cone_acc[rc] += dot(lv, pats[slot]) + dot(rv, pats[3 - slot])
            for rows, ln in pieces(c * CH, (c + 1) * CH):
                fv = f[rows, ln]
                grad = lin[rows, ln] + fv + (fv - cone_acc[rows, ln])
                fv = jnp.clip(fv - 0.4 * grad, 0.0, 1.0)
                f[rows, ln] = fv
                if s < STEPS - 1 or s % 2:
                    hi = fv.astype(BF16)
                    rounded[s + 1, rows, ln] = hi
                    if s % 2:
                        low[rows, ln] = (fv - hi.astype(F32)).astype(BF16)
            if s < STEPS - 1:
                start_halo(s + 1, c)
            else:
                for i in range(c * nc // NCH, (c + 1) * nc // NCH):
                    snd_o[i] = to16(fold((f[i * UNIT:(i + 1) * UNIT] - 0.5) * FRAC_CODE))
        if s < STEPS - 1:
            cone_acc[...] = dot(rounded[s + 1], pats[0])

    step(0)
    step(1)
    cen = average(2)
    gain[...] = f[...] - cen
    lin[...] = lin_next(lin, gain, cen, rcv_l, nc)
    step(2)
    step(3)
    send_all(snd_o, rcv_o, 2)
    rcv_o[sc] = snd_o[sc]
    cen = average(4)
    gain[...] += f[...] - cen
    for i in range(nc):
        snd_d[i] = to16(fold(gain[i * UNIT:(i + 1) * UNIT] * GAIN_CODE))
    send_all(snd_d, rcv_d, 3)
    rcv_d[sc] = snd_d[sc]

    def home(rcv, t):
        v = jnp.concatenate([from16(rcv[g * TL + t]) for g in range(nc // TL)], axis=0)
        parts = []
        for h in range(2):
            half = jnp.concatenate(
                [v[(2 * g + h) * UNIT:(2 * g + h + 1) * UNIT] for g in range(nc // TL)], axis=0)
            hi, lo = split(half)
            parts.append(dot(back[...], hi) + dot(back[...], lo))
        return jnp.concatenate(parts, axis=1)

    outs = []
    wait_all(rcv_o, a_recv, 2)
    for t in range(TL):
        ln = slice(t * TILE, (t + 1) * TILE)
        out_f[:, ln] = home(rcv_o, t) * (1.0 / FRAC_CODE) + 0.5
    outs.append(pltpu.make_async_copy(out_f, f_out, out_sem.at[0]))
    outs[-1].start()
    wait_all(rcv_d, a_recv, 3)
    for t in range(TL):
        ln = slice(t * TILE, (t + 1) * TILE)
        out_d[:, ln] = dual_v[:, ln] + home(rcv_d, t) * (1.0 / GAIN_CODE)
    outs.append(pltpu.make_async_copy(out_d, d_out, out_sem.at[1]))
    outs[-1].start()
    for o in outs:
        o.wait()
    for k, buf in enumerate((snd_f, snd_l, snd_o, snd_d)):
        wait_all(buf, a_send, k)
    for s in range(STEPS):
        for side in range(2):
            part = halo.at[s, side]
            pltpu.make_async_copy(part, part, halo_send.at[s, side]).wait()


def lin_next(lin, gain, cen, rcv_l, nc):
    v = [from16(rcv_l[i]) * (1.0 / LIN_CODE) for i in range(nc)]
    v = jnp.concatenate([jnp.concatenate([u[:UNIT], u[UNIT:]], axis=1) for u in v], axis=0)
    return v + gain[...] - cen


def body(start_fraction, ore_value, dual_price, patterns, cone_list, node_list, probability):
    ns, nc = lax.axis_size("space"), lax.axis_size("scen")
    blocks = start_fraction.shape[2]
    flat = (HOME, blocks)
    hbm = pl.BlockSpec(memory_space=pltpu.HBM)
    dma = pltpu.SemaphoreType.DMA
    v = pltpu.VMEM
    f, d = pl.pallas_call(
        functools.partial(kernel, ns, nc),
        out_shape=[jax.ShapeDtypeStruct(flat, F32)] * 2,
        in_specs=[hbm] * 7,
        out_specs=[hbm] * 2,
        scratch_shapes=[
            pltpu.SMEM((TL, 3), jnp.int32),
            v((2, SCEN), jnp.int32),
            v((1, SCEN), F32),
            v(flat, BF16),
            v(flat, BF16),
            v(flat, F32),
            v((3, TILE, TILE), BF16),
            v((HOME, HOME), BF16),
            v((HOME, HOME), BF16),
            v((2, ROWS, ROWS), BF16),
            v((STEPS + 1, ROWS, TILE), BF16),
            v((STEPS, 2, ROWS, TILE), BF16),
            v((ROWS, TILE), F32),
            v((ROWS, TILE), BF16),
            v((ROWS, TILE), F32),
            v((ROWS, TILE), F32),
            v((ROWS, TILE), F32),
            v((nc, *MSG), BF16),
            v((nc, *MSG), BF16),
            v((nc, *MSG), I16),
            v((nc, *MSG), I16),
            v((nc, *MSG), I16),
            v((nc, *MSG), I16),
            v((nc, *MSG), I16),
            v((nc, *MSG), I16),
            v(flat, F32),
            v(flat, F32),
            dma((7,)),
            dma((2,)),
            dma((STEPS, 2)),
            dma((STEPS, 2, NCH)),
            dma((4,)),
            dma((4,)),
            dma((1,)),
        ],
        compiler_params=pltpu.CompilerParams(
            collective_id=0, has_side_effects=True, vmem_limit_bytes=56 * 2**20
        ),
    )(
        cone_list,
        node_list,
        probability.reshape(1, -1),
        start_fraction.reshape(flat),
        ore_value.reshape(flat),
        dual_price.reshape(flat),
        patterns,
    )
    return f.reshape(start_fraction.shape), d.reshape(start_fraction.shape)


def solution(mesh):
    in_specs = (
        P("scen", None, "space"),
        P("scen", None, "space"),
        P("scen", None, "space"),
        P(),
        P("space", None),
        P(),
        P(),
    )
    out_specs = (P("scen", None, "space"), P("scen", None, "space"))
    return jax.shard_map(body, mesh=mesh, in_specs=in_specs, out_specs=out_specs, check_vma=False)
```

```python
import functools

import jax
import jax.numpy as jnp
from jax import lax
from jax.experimental import pallas as pl
from jax.experimental.pallas import tpu as pltpu
from jax.sharding import PartitionSpec as P

TILE = 512
STEPS = 4
F32 = jnp.float32
BF16 = jnp.bfloat16
I16 = jnp.int16
MESH = pl.DeviceIdType.MESH

SCEN = 64
SCL = 4
PER = 24
HOME = SCL * PER
TL = 4
GRP = 3
HALF = TILE // 2
MAIN, EXTRA = 4, 2
UNITS = MAIN + EXTRA
RUNS = ((0, MAIN), (MAIN, UNITS))
ROWS = MAIN * SCL
LIN_CODE = 32767.0 / 9.0
FRAC_CODE = 65534.0
GAIN_CODE = 32767.0 / 2.0


def iota(shape, dim):
    return lax.broadcasted_iota(jnp.int32, shape, dim)


def div(r, by, most):
    mul = (1 << 16) // by + 1
    assert all((v * mul) >> 16 == v // by for v in range(most))
    return (r * mul) >> 16


def split(x):
    hi = x.astype(BF16)
    return hi, (x - hi.astype(F32)).astype(BF16)


def round16(x):
    return jnp.round(x).astype(jnp.int32)


def wide(v):
    return v.astype(F32) if v.dtype == BF16 else v.astype(jnp.int32).astype(F32)


def dot(a, b):
    return jnp.dot(a, b, preferred_element_type=F32)


def dot_0(a, b):
    return lax.dot_general(a, b, (((0,), (0,)), ((), ())), preferred_element_type=F32)


def fold(x):
    return jnp.concatenate([x[:, :HALF], x[:, HALF:]], axis=0)


def unfold(x):
    h = ROWS // 2
    return jnp.concatenate([x[:h], x[h:]], axis=1)


def kernel(ns, nc, cone_in, node_in, prob_in, start, ore, dual, pats_in, out_f, out_d,
           cone, node, prob_v, f0_v, ore_v, dual_v, pats, perm, back, order, mean,
           rounded, halo, f, low, lin, gain, cone_acc,
           snd_f, rcv_f, snd_l, rcv_l, snd_o, rcv_o, snd_d, rcv_d,
           snd_fe, rcv_fe, snd_le, rcv_le, snd_oe, rcv_oe, snd_de, rcv_de, cone_v,
           load_sem, halo_send, halo_recv, a_send, a_recv, cone_sem):
    sp = lax.axis_index("space")
    sc = lax.axis_index("scen")
    z, yh = lax.div(sp, 2), lax.rem(sp, 2)
    x, yl, core = lax.div(sc, 4), lax.rem(lax.div(sc, 2), 2), lax.rem(sc, 2)
    odd = lax.rem(z, 2)
    half = lax.rem(yl + odd, 2)
    y_own = lax.rem(yh + odd, 2)
    main_slot = (2 * x + yh) * 2 + yl
    extra_slot = (2 * x + yh) * 2 + core
    main_home = core == yh
    extra_home = half == yh
    near = (sp, sc + 1 - 2 * core)
    over = (jnp.where(core == 0, lax.rem(sp + ns - 2, ns), lax.rem(sp + 2, ns)), near[1])
    inside = half != core
    far = (over, (jnp.where(inside, sp, over[0]), jnp.where(inside, 4 * x + 2 * (1 - yl) + 1 - core, over[1])))

    barrier = pltpu.get_barrier_semaphore()
    for nb in (near, over):
        pl.semaphore_signal(barrier, inc=1, device_id=nb, device_id_type=MESH)

    @pl.loop(1, 2 * nc)
    def _(d):
        k = lax.rem(yh * nc + sc + d, 2 * nc)
        pl.semaphore_signal(barrier, inc=1, device_id=(2 * z + lax.div(k, nc), lax.rem(k, nc)), device_id_type=MESH)

    def load(k, src, dst):
        c = pltpu.make_async_copy(src, dst, load_sem.at[k])
        c.start()
        return c

    load_f0 = load(0, start, f0_v)
    load_ore = load(1, ore, ore_v)
    load_dual = load(2, dual, dual_v)
    load_node = load(3, node_in, node)
    load_prob = load(4, prob_in, prob_v)
    load_cone = load(5, cone_in, cone_v.at[0])
    load_pats = load(6, pats_in, pats)

    def places(home_dim):
        n = TL * HOME
        shape = (n, n)
        h, g = iota(shape, home_dim), iota(shape, 1 - home_dim)
        if home_dim:
            h1 = iota((1, n), 1)
        else:
            h1 = iota((n, 1), 0)
        tile = div(h1, HOME, n)
        hr = h1 - HOME * tile
        hs = div(hr, PER, HOME)
        hp = hr - PER * hs
        hg = div(hp, GRP, PER)
        which = hp - GRP * hg
        at_main = (hg * 2 + (which >> 1)) * ROWS + tile * SCL + hs
        at_extra = nc * ROWS + hg * ROWS + tile * SCL + hs
        return jnp.where(jnp.where(which == 1, at_extra, at_main) == g, 1.0, 0.0).astype(BF16)

    perm[...] = places(1)
    back[...] = places(0)

    n = SCEN * MAIN
    q, g = iota((n, 1), 0), iota((1, n), 1)
    order_m = jnp.where(
        ((q & (SCEN - 1)) >> 2) * ROWS + (q >> 6) * SCL + (q & 3) == g, 1.0, 0.0).astype(BF16)
    q, g = iota((n // 2, 1), 0), iota((1, n // 2), 1)
    order_e = jnp.where(
        ((q & (SCEN - 1)) >> 2) * (ROWS // 2) + (q >> 6) * SCL + (q & 3) == g, 1.0, 0.0).astype(BF16)

    bufs = (
        ((snd_f, rcv_f), (snd_fe, rcv_fe)),
        ((snd_l, rcv_l), (snd_le, rcv_le)),
        ((snd_o, rcv_o), (snd_oe, rcv_oe)),
        ((snd_d, rcv_d), (snd_de, rcv_de)),
    )

    def send(skip, own, src, dst, mine, k, device):
        @pl.loop(0, nc)
        def _(d):
            m = lax.rem(own + 1 + d, nc)

            @pl.when(jnp.logical_not(skip & (m == own)))
            def _():
                pltpu.make_async_remote_copy(
                    src.at[m], dst.at[mine], a_send.at[k], a_recv.at[k],
                    device_id=device(m), device_id_type=MESH).start()

        @pl.when(skip)
        def _():
            dst[mine] = src[own]

    def main_owner(m):
        g = lax.div(m, 2)
        return 2 * z + lax.rem(g, 2), 4 * lax.div(g, 2) + 2 * lax.rem(m, 2) + yh

    def extra_owner(m):
        g = lax.div(m, 2)
        return 2 * z + lax.rem(g, 2), 4 * lax.div(g, 2) + 2 * y_own + lax.rem(m, 2)

    def send_out(k, e):
        if e:
            send(extra_home, extra_slot, *bufs[k][1], sc, 2 * k + 1, extra_owner)
        else:
            send(main_home, main_slot, *bufs[k][0], sc, 2 * k, main_owner)

    def send_back(k, e):
        if e:
            send(extra_home, sc, *bufs[k][1], extra_slot, 2 * k + 1, lambda i: (2 * z + half, i))
        else:
            send(main_home, sc, *bufs[k][0], main_slot, 2 * k, lambda i: (2 * z + core, i))

    def wait_all(k, e, sem, buf):
        kept = (main_home, extra_home)[e]

        @pl.when(kept)
        def _():
            part = buf.at[pl.ds(0, nc - 1)]
            pltpu.make_async_copy(part, part, sem.at[2 * k + e]).wait()

        @pl.when(jnp.logical_not(kept))
        def _():
            pltpu.make_async_copy(buf, buf, sem.at[2 * k + e]).wait()

    def pack(snd, snd_e, terms, encode):
        m = encode(sum(dot(perm[...], term) for term in terms))
        n = nc * ROWS
        snd[...] = m[:n].astype(snd.dtype).reshape(nc, ROWS, TILE)
        for j in range(nc):
            snd_e[j] = fold(m[n + 8 * j:n + 8 * j + 8]).astype(snd.dtype)

    def tiles(fn):
        return jnp.concatenate([fn(slice(t * TILE, (t + 1) * TILE)) for t in range(TL)], axis=0)

    load_f0.wait()
    pack(snd_f, snd_fe, [tiles(lambda ln: f0_v[:, ln])], lambda v: v)
    load_ore.wait()
    load_dual.wait()

    lin_home = tiles(lambda ln: jnp.round((dual_v[:, ln] - ore_v[:, ln].astype(F32)) * LIN_CODE))
    pack(snd_l, snd_le, split(lin_home), round16)
    load_node.wait()
    load_prob.wait()
    prob = prob_v[...]
    nodes = jnp.where(x == 2, node[1:2, :], node[0:1, :])
    onehot = jnp.where(iota((16, SCEN), 0) == nodes, 1.0, 0.0)
    same = lax.dot_general(onehot.T.astype(BF16), onehot.astype(BF16), (((1,), (0,)), ((), ())),
                           preferred_element_type=F32)
    eye = jnp.where(iota((SCEN, SCEN), 0) == iota((SCEN, SCEN), 1), 1.0, 0.0)
    same = jnp.where(x == 0, jnp.ones_like(same), jnp.where(x == 3, eye, same))
    raw = same * prob
    m = raw / jnp.sum(raw, axis=1, keepdims=True)
    for k, part in enumerate(split(m)):
        mean[k] = part
    for s in range(STEPS):
        rounded[s, UNITS] = jnp.zeros((SCEN, TILE), BF16)
    order[...] = order_m

    pl.semaphore_wait(barrier, 2 * nc + 1)
    for e in (1, 0):
        for k in range(2):
            send_out(k, e)
    load_cone.wait()
    cone_copy = pltpu.make_async_remote_copy(
        cone_v.at[0], cone_v.at[1], cone_sem.at[0], cone_sem.at[1],
        device_id=(2 * z + 1 - yh, sc), device_id_type=MESH)
    cone_copy.start()

    def start_halo(step, e, u, side, to):
        pltpu.make_async_remote_copy(
            rounded.at[step, u], halo.at[step, e, 1 - side],
            halo_send.at[step, e, side], halo_recv.at[step, e, 1 - side],
            device_id=to, device_id_type=MESH).start()

    ends = [(e, core, (MAIN + core if e else (MAIN - 1) * core), far[e]) for e in range(2)]
    ends += [(e, 1 - core, (MAIN + 1 - core if e else (MAIN - 1) * (1 - core)), near) for e in range(2)]

    ends = [[end for end in ends[2:] + ends[:2] if end[0] == e] for e in range(2)]

    def received(k, e):
        wait_all(k, e, a_recv, bufs[k][e][1])
        rcv = bufs[k][e][1]
        if e:
            v = jnp.concatenate([unfold(wide(rcv[i])) for i in range(nc)], axis=0)
        else:
            v = wide(rcv[...].reshape(nc * ROWS, TILE))
        terms = split(v) if k else (v.astype(BF16),)
        v = sum(dot(order_e if e else order[...], term) for term in terms)
        first, last = RUNS[e]
        return {u: v[(u - first) * SCEN:(u - first + 1) * SCEN] for u in range(first, last)}

    def take_fraction(e):
        for u, fv in received(0, e).items():
            f[u] = fv
            rounded[0, u] = fv.astype(BF16)
        for _, side, u, to in ends[e][::-1]:
            start_halo(0, e, u, side, to)

    take_fraction(1)
    cone_copy.wait()
    cone_loads = [pltpu.make_async_copy(cone_v.at[k], cone.at[k], cone_sem.at[2 + k]) for k in range(2)]
    for c in cone_loads:
        c.start()
    for c in cone_loads:
        c.wait()
    load_pats.wait()
    tile, lslot = [], []
    for u in range(UNITS):
        run, at = (core, u) if u < MAIN else (half, 2 * core + u - MAIN)
        tile.append((2 * z + run) * TL + at)
        lslot.append(jnp.where(cone[jnp.where(run == yh, 0, 1), at, 1] == jnp.maximum(tile[u] - 1, 0), 1, 2))

    def average(step, u):
        hi = rounded[step, u]
        c = dot(mean[0], hi) + dot(mean[1], hi)
        return c if step == 0 else c + dot(mean[0], low[u])

    def cone_own(e, step):
        first, last = RUNS[e]
        n = last - first
        acc = dot(rounded[step, first:last].reshape(n * SCEN, TILE), pats[0])
        for k in (1, 2):
            picked = []
            for u in range(first, last):
                to_left = UNITS if u == first else u - 1
                to_right = UNITS if u == last - 1 else u + 1
                picked.append(rounded[step, jnp.where(lslot[u] == k, to_left, to_right)])
            acc = acc + dot(jnp.concatenate(picked, axis=0), pats[k])
        cone_acc[first:last] = acc.reshape(n, SCEN, TILE)

    def first_center(e):
        for u in range(*RUNS[e]):
            gain[u] = average(0, u)
        cone_own(e, 0)

    def take_linear(e):
        for u, lv in received(1, e).items():
            lin[u] = lv * (1.0 / LIN_CODE) - gain[u]

    def descend(s, u):
        for q in range(TILE // 128):
            ln = slice(q * 128, (q + 1) * 128)
            fv = f[u, :, ln]
            grad = lin[u, :, ln] + fv + (fv - cone_acc[u, :, ln])
            fv = jnp.clip(fv - 0.4 * grad, 0.0, 1.0)
            f[u, :, ln] = fv
            hi = fv.astype(BF16)
            rounded[s + 1, u, :, ln] = hi
            if s % 2:
                low[u, :, ln] = (fv - hi.astype(F32)).astype(BF16)

    def step(e, s):
        first, last = RUNS[e]
        for u in range(first + 1, last - 1):
            descend(s, u)
        for _, side, u, to in ends[e]:
            here = halo.at[s, e, side]
            pltpu.make_async_copy(here, here, halo_recv.at[s, e, side]).wait()
            at_end = jnp.where(side == 0, tile[first] == 0, tile[last - 1] == ns * TL - 1)
            slot = jnp.where(side == 0, lslot[first], 3 - lslot[last - 1])
            away = jnp.where(at_end, rounded[s, u], halo[s, e, side])
            cone_acc[u] += dot(away, pats[slot])
            descend(s, u)
            if s < STEPS - 1:
                start_halo(s + 1, e, u, side, to)
        if s < STEPS - 1:
            cone_own(e, s + 1)
        if s == 1:
            for u in range(first, last):
                cen = average(2, u)
                up = f[u] - cen
                lin[u] = lin[u] + gain[u] + up - cen
                gain[u] = up

    def pack_back(k, e, values):
        v = jnp.concatenate([round16(values(u)).astype(F32) for u in range(*RUNS[e])], axis=0)
        v = round16(sum(dot_0(order_e if e else order[...], term) for term in split(v)))
        snd = bufs[k][e][0]
        if e:
            for i in range(nc):
                snd[i] = fold(v[8 * i:8 * i + 8]).astype(I16)
        else:
            snd[...] = v.astype(I16).reshape(nc, ROWS, TILE)
        send_back(k, e)

    def give_back(e):
        pack_back(2, e, lambda u: (f[u] - 0.5) * FRAC_CODE)
        for u in range(*RUNS[e]):
            gain[u] += f[u] - average(4, u)
        pack_back(3, e, lambda u: gain[u] * GAIN_CODE)

    first_center(1)
    take_linear(1)
    step(1, 0)
    take_fraction(0)
    first_center(0)
    step(1, 1)
    take_linear(0)
    step(0, 0)
    step(1, 2)
    step(0, 1)
    step(1, 3)
    give_back(1)
    step(0, 2)
    step(0, 3)
    give_back(0)

    def home(k, e, write):
        wait_all(k, e, a_recv, bufs[k][e][1])
        rcv = bufs[k][e][1]
        n = nc * ROWS
        if e:
            v = jnp.concatenate([unfold(wide(rcv[j])) for j in range(nc)], axis=0)
            mat = back[:, n:]
        else:
            v = wide(rcv[...].reshape(n, TILE))
            mat = back[:, :n]
        m = sum(dot(mat, term) for term in split(v))
        for t in range(TL):
            write(slice(t * TILE, (t + 1) * TILE), m[t * HOME:(t + 1) * HOME])

    def write_f(ln, m):
        out_f[:, ln] = m * (1.0 / FRAC_CODE) + 0.5

    def write_d(ln, m):
        out_d[:, ln] = dual_v[:, ln] + m * (1.0 / GAIN_CODE)

    def add_f(ln, m):
        out_f[:, ln] += m * (1.0 / FRAC_CODE)

    def add_d(ln, m):
        out_d[:, ln] += m * (1.0 / GAIN_CODE)

    home(2, 1, write_f)
    home(3, 1, write_d)
    home(2, 0, add_f)
    home(3, 0, add_d)
    for k in range(4):
        for e in range(2):
            wait_all(k, e, a_send, bufs[k][e][0])
    for s in range(STEPS):
        for e in range(2):
            for side in range(2):
                part = halo.at[s, e, side]
                pltpu.make_async_copy(part, part, halo_send.at[s, e, side]).wait()


def body(start_fraction, ore_value, dual_price, patterns, cone_list, node_list, probability):
    ns, nc = lax.axis_size("space"), lax.axis_size("scen")
    blocks = start_fraction.shape[2]
    flat = (HOME, blocks)
    hbm = pl.BlockSpec(memory_space=pltpu.HBM)
    dma = pltpu.SemaphoreType.DMA
    v = pltpu.VMEM
    f, d = pl.pallas_call(
        functools.partial(kernel, ns, nc),
        out_shape=[v(flat, F32)] * 2,
        in_specs=[hbm] * 7,
        out_specs=[pl.BlockSpec(memory_space=v)] * 2,
        scratch_shapes=[
            pltpu.SMEM((2, TL, 3), jnp.int32),
            v((2, SCEN), jnp.int32),
            v((1, SCEN), F32),
            v(flat, BF16),
            v(flat, BF16),
            v(flat, F32),
            v((3, TILE, TILE), BF16),
            v((TL * HOME, TL * HOME), BF16),
            v((TL * HOME, TL * HOME), BF16),
            v((SCEN * MAIN, SCEN * MAIN), BF16),
            v((2, SCEN, SCEN), BF16),
            v((STEPS + 1, UNITS + 1, SCEN, TILE), BF16),
            v((STEPS, 2, 2, SCEN, TILE), BF16),
            v((UNITS, SCEN, TILE), F32),
            v((UNITS, SCEN, TILE), BF16),
            v((UNITS, SCEN, TILE), F32),
            v((UNITS, SCEN, TILE), F32),
            v((UNITS, SCEN, TILE), F32),
            *[v((nc, ROWS, TILE), kind) for kind in (BF16, BF16, *[I16] * 6)],
            *[v((nc, ROWS, HALF), kind) for kind in (BF16, BF16, *[I16] * 6)],
            v((2, TL, 3), jnp.int32),
            dma((7,)),
            dma((STEPS, 2, 2)),
            dma((STEPS, 2, 2)),
            dma((8,)),
            dma((8,)),
            dma((4,)),
        ],
        compiler_params=pltpu.CompilerParams(
            collective_id=0, has_side_effects=True, vmem_limit_bytes=56 * 2**20
        ),
    )(
        cone_list,
        node_list,
        probability.reshape(1, -1),
        start_fraction.reshape(flat),
        ore_value.reshape(flat),
        dual_price.reshape(flat),
        patterns,
    )
    return f.reshape(start_fraction.shape), d.reshape(start_fraction.shape)


def solution(mesh):
    in_specs = (
        P("scen", None, "space"),
        P("scen", None, "space"),
        P("scen", None, "space"),
        P(),
        P("space", None),
        P(),
        P(),
    )
    out_specs = (P("scen", None, "space"), P("scen", None, "space"))
    return jax.shard_map(body, mesh=mesh, in_specs=in_specs, out_specs=out_specs, check_vma=False)
```

```python
import functools

import jax
import jax.numpy as jnp
from jax import lax
from jax.experimental import pallas as pl
from jax.experimental.pallas import tpu as pltpu
from jax.sharding import PartitionSpec as P

TILE = 512
STEPS = 4
F32 = jnp.float32
BF16 = jnp.bfloat16
I16 = jnp.int16
MESH = pl.DeviceIdType.MESH

SCEN = 64
SCL = 4
PER = 24
HOME = SCL * PER
TL = 4
GRP = 3
HALF = TILE // 2
MAIN, EXTRA = 4, 2
UNITS = MAIN + EXTRA
RUNS = ((0, MAIN), (MAIN, UNITS))
ROWS = MAIN * SCL
LIN_CODE = 32767.0 / 9.0
FRAC_CODE = 65534.0
GAIN_CODE = 32767.0 / 2.0


def iota(shape, dim):
    return lax.broadcasted_iota(jnp.int32, shape, dim)


def div(r, by, most):
    mul = (1 << 16) // by + 1
    assert all((v * mul) >> 16 == v // by for v in range(most))
    return (r * mul) >> 16


def split(x):
    hi = x.astype(BF16)
    return hi, (x - hi.astype(F32)).astype(BF16)


def round16(x):
    return jnp.round(x).astype(jnp.int32)


def wide(v):
    return v.astype(F32) if v.dtype == BF16 else v.astype(jnp.int32).astype(F32)


def dot(a, b):
    return jnp.dot(a, b, preferred_element_type=F32)


def dot_0(a, b):
    return lax.dot_general(a, b, (((0,), (0,)), ((), ())), preferred_element_type=F32)


def fold(x):
    return jnp.concatenate([x[:, :HALF], x[:, HALF:]], axis=0)


def unfold(x):
    h = ROWS // 2
    return jnp.concatenate([x[:h], x[h:]], axis=1)


def kernel(ns, nc, cone_in, node_in, prob_in, start, ore, dual, pats_in, out_f, out_d,
           cone, node, prob_v, f0_v, ore_v, dual_v, pats, perm, back, order, mean,
           rounded, halo, f, low, lin, gain, cone_acc,
           snd_f, rcv_f, snd_l, rcv_l, snd_o, rcv_o, snd_d, rcv_d,
           snd_fe, rcv_fe, snd_le, rcv_le, snd_oe, rcv_oe, snd_de, rcv_de, cone_v,
           load_sem, halo_send, halo_recv, a_send, a_recv, cone_sem):
    sp = lax.axis_index("space")
    sc = lax.axis_index("scen")
    z, yh = lax.div(sp, 2), lax.rem(sp, 2)
    x, yl, core = lax.div(sc, 4), lax.rem(lax.div(sc, 2), 2), lax.rem(sc, 2)
    odd = lax.rem(z, 2)
    half = lax.rem(yl + odd, 2)
    y_own = lax.rem(yh + odd, 2)
    main_slot = (2 * x + yh) * 2 + yl
    extra_slot = (2 * x + yh) * 2 + core
    main_home = core == yh
    extra_home = half == yh
    near = (sp, sc + 1 - 2 * core)
    over = (jnp.where(core == 0, lax.rem(sp + ns - 2, ns), lax.rem(sp + 2, ns)), near[1])
    inside = half != core
    far = (over, (jnp.where(inside, sp, over[0]), jnp.where(inside, 4 * x + 2 * (1 - yl) + 1 - core, over[1])))

    barrier = pltpu.get_barrier_semaphore()
    for nb in (near, over):
        pl.semaphore_signal(barrier, inc=1, device_id=nb, device_id_type=MESH)

    @pl.loop(1, 2 * nc)
    def _(d):
        k = lax.rem(yh * nc + sc + d, 2 * nc)
        pl.semaphore_signal(barrier, inc=1, device_id=(2 * z + lax.div(k, nc), lax.rem(k, nc)), device_id_type=MESH)

    def load(k, src, dst):
        c = pltpu.make_async_copy(src, dst, load_sem.at[k])
        c.start()
        return c

    load_f0 = load(0, start, f0_v)
    load_ore = load(1, ore, ore_v)
    load_dual = load(2, dual, dual_v)
    load_node = load(3, node_in, node)
    load_prob = load(4, prob_in, prob_v)
    load_cone = load(5, cone_in, cone_v.at[0])
    load_pats = load(6, pats_in, pats)

    def places(home_dim):
        n = TL * HOME
        shape = (n, n)
        h, g = iota(shape, home_dim), iota(shape, 1 - home_dim)
        if home_dim:
            h1 = iota((1, n), 1)
        else:
            h1 = iota((n, 1), 0)
        tile = div(h1, HOME, n)
        hr = h1 - HOME * tile
        hs = div(hr, PER, HOME)
        hp = hr - PER * hs
        hg = div(hp, GRP, PER)
        which = hp - GRP * hg
        at_main = (hg * 2 + (which >> 1)) * ROWS + tile * SCL + hs
        at_extra = nc * ROWS + hg * ROWS + tile * SCL + hs
        return jnp.where(jnp.where(which == 1, at_extra, at_main) == g, 1.0, 0.0).astype(BF16)

    perm[...] = places(1)

    bufs = (
        ((snd_f, rcv_f), (snd_fe, rcv_fe)),
        ((snd_l, rcv_l), (snd_le, rcv_le)),
        ((snd_o, rcv_o), (snd_oe, rcv_oe)),
        ((snd_d, rcv_d), (snd_de, rcv_de)),
    )

    def send(skip, own, src, dst, mine, k, device):
        @pl.loop(0, nc)
        def _(d):
            m = lax.rem(own + 1 + d, nc)

            @pl.when(jnp.logical_not(skip & (m == own)))
            def _():
                pltpu.make_async_remote_copy(
                    src.at[m], dst.at[mine], a_send.at[k], a_recv.at[k],
                    device_id=device(m), device_id_type=MESH).start()

        @pl.when(skip)
        def _():
            dst[mine] = src[own]

    def main_owner(m):
        g = lax.div(m, 2)
        return 2 * z + lax.rem(g, 2), 4 * lax.div(g, 2) + 2 * lax.rem(m, 2) + yh

    def extra_owner(m):
        g = lax.div(m, 2)
        return 2 * z + lax.rem(g, 2), 4 * lax.div(g, 2) + 2 * y_own + lax.rem(m, 2)

    def send_out(k, e):
        if e:
            send(extra_home, extra_slot, *bufs[k][1], sc, 2 * k + 1, extra_owner)
        else:
            send(main_home, main_slot, *bufs[k][0], sc, 2 * k, main_owner)

    def send_back(k, e):
        if e:
            send(extra_home, sc, *bufs[k][1], extra_slot, 2 * k + 1, lambda i: (2 * z + half, i))
        else:
            send(main_home, sc, *bufs[k][0], main_slot, 2 * k, lambda i: (2 * z + core, i))

    def wait_all(k, e, sem, buf):
        kept = (main_home, extra_home)[e]

        @pl.when(kept)
        def _():
            part = buf.at[pl.ds(0, nc - 1)]
            pltpu.make_async_copy(part, part, sem.at[2 * k + e]).wait()

        @pl.when(jnp.logical_not(kept))
        def _():
            pltpu.make_async_copy(buf, buf, sem.at[2 * k + e]).wait()

    def pack(snd, snd_e, terms, encode):
        m = encode(sum(dot(perm[...], term) for term in terms))
        n = nc * ROWS
        snd[...] = m[:n].astype(snd.dtype).reshape(nc, ROWS, TILE)
        for j in range(nc):
            snd_e[j] = fold(m[n + 8 * j:n + 8 * j + 8]).astype(snd.dtype)

    def tiles(fn):
        return jnp.concatenate([fn(slice(t * TILE, (t + 1) * TILE)) for t in range(TL)], axis=0)

    load_f0.wait()
    pack(snd_f, snd_fe, [tiles(lambda ln: f0_v[:, ln])], lambda v: v)
    pl.semaphore_wait(barrier, 2 * nc + 1)
    send_out(0, 1)
    send_out(0, 0)
    load_cone.wait()
    cone_copy = pltpu.make_async_remote_copy(
        cone_v.at[0], cone_v.at[1], cone_sem.at[0], cone_sem.at[1],
        device_id=(2 * z + 1 - yh, sc), device_id_type=MESH)
    cone_copy.start()

    load_ore.wait()
    load_dual.wait()

    lin_home = tiles(lambda ln: jnp.round((dual_v[:, ln] - ore_v[:, ln].astype(F32)) * LIN_CODE))
    pack(snd_l, snd_le, split(lin_home), round16)
    send_out(1, 1)
    send_out(1, 0)
    load_node.wait()
    load_prob.wait()
    prob = prob_v[...]
    nodes = jnp.where(x == 2, node[1:2, :], node[0:1, :])
    onehot = jnp.where(iota((16, SCEN), 0) == nodes, 1.0, 0.0)
    same = lax.dot_general(onehot.T.astype(BF16), onehot.astype(BF16), (((1,), (0,)), ((), ())),
                           preferred_element_type=F32)
    eye = jnp.where(iota((SCEN, SCEN), 0) == iota((SCEN, SCEN), 1), 1.0, 0.0)
    same = jnp.where(x == 0, jnp.ones_like(same), jnp.where(x == 3, eye, same))
    raw = same * prob
    m = raw / jnp.sum(raw, axis=1, keepdims=True)
    for k, part in enumerate(split(m)):
        mean[k] = part
    for s in range(STEPS):
        rounded[s, UNITS] = jnp.zeros((SCEN, TILE), BF16)
    n = SCEN * MAIN
    q, g = iota((n, 1), 0), iota((1, n), 1)
    order_m = jnp.where(
        ((q & (SCEN - 1)) >> 2) * ROWS + (q >> 6) * SCL + (q & 3) == g, 1.0, 0.0).astype(BF16)
    q, g = iota((n // 2, 1), 0), iota((1, n // 2), 1)
    order_e = jnp.where(
        ((q & (SCEN - 1)) >> 2) * (ROWS // 2) + (q >> 6) * SCL + (q & 3) == g, 1.0, 0.0).astype(BF16)

    order[...] = order_m
    back[...] = places(0)

    def start_halo(step, e, u, side, to):
        pltpu.make_async_remote_copy(
            rounded.at[step, u], halo.at[step, e, 1 - side],
            halo_send.at[step, e, side], halo_recv.at[step, e, 1 - side],
            device_id=to, device_id_type=MESH).start()

    ends = [(e, core, (MAIN + core if e else (MAIN - 1) * core), far[e]) for e in range(2)]
    ends += [(e, 1 - core, (MAIN + 1 - core if e else (MAIN - 1) * (1 - core)), near) for e in range(2)]

    ends = [[end for end in ends[2:] + ends[:2] if end[0] == e] for e in range(2)]

    def received(k, e):
        wait_all(k, e, a_recv, bufs[k][e][1])
        rcv = bufs[k][e][1]
        if e:
            v = jnp.concatenate([unfold(wide(rcv[i])) for i in range(nc)], axis=0)
        else:
            v = wide(rcv[...].reshape(nc * ROWS, TILE))
        terms = split(v) if k else (v.astype(BF16),)
        v = sum(dot(order_e if e else order[...], term) for term in terms)
        first, last = RUNS[e]
        return {u: v[(u - first) * SCEN:(u - first + 1) * SCEN] for u in range(first, last)}

    def take_fraction(e):
        for u, fv in received(0, e).items():
            f[u] = fv
            rounded[0, u] = fv.astype(BF16)
        for _, side, u, to in ends[e][::-1]:
            start_halo(0, e, u, side, to)

    take_fraction(1)
    cone_copy.wait()
    cone_loads = [pltpu.make_async_copy(cone_v.at[k], cone.at[k], cone_sem.at[2 + k]) for k in range(2)]
    for c in cone_loads:
        c.start()
    for c in cone_loads:
        c.wait()
    load_pats.wait()
    tile, lslot = [], []
    for u in range(UNITS):
        run, at = (core, u) if u < MAIN else (half, 2 * core + u - MAIN)
        tile.append((2 * z + run) * TL + at)
        lslot.append(jnp.where(cone[jnp.where(run == yh, 0, 1), at, 1] == jnp.maximum(tile[u] - 1, 0), 1, 2))

    def average(step, u):
        hi = rounded[step, u]
        c = dot(mean[0], hi) + dot(mean[1], hi)
        return c if step == 0 else c + dot(mean[0], low[u])

    def cone_own(e, step):
        first, last = RUNS[e]
        n = last - first
        acc = dot(rounded[step, first:last].reshape(n * SCEN, TILE), pats[0])
        for k in (1, 2):
            picked = []
            for u in range(first, last):
                to_left = UNITS if u == first else u - 1
                to_right = UNITS if u == last - 1 else u + 1
                picked.append(rounded[step, jnp.where(lslot[u] == k, to_left, to_right)])
            acc = acc + dot(jnp.concatenate(picked, axis=0), pats[k])
        cone_acc[first:last] = acc.reshape(n, SCEN, TILE)

    def first_center(e):
        for u in range(*RUNS[e]):
            gain[u] = average(0, u)
        cone_own(e, 0)

    def take_linear(e):
        for u, lv in received(1, e).items():
            lin[u] = lv * (1.0 / LIN_CODE) - gain[u]

    def descend(s, u):
        for q in range(TILE // 128):
            ln = slice(q * 128, (q + 1) * 128)
            fv = f[u, :, ln]
            grad = lin[u, :, ln] + fv + (fv - cone_acc[u, :, ln])
            fv = jnp.clip(fv - 0.4 * grad, 0.0, 1.0)
            f[u, :, ln] = fv
            hi = fv.astype(BF16)
            rounded[s + 1, u, :, ln] = hi
            if s % 2:
                low[u, :, ln] = (fv - hi.astype(F32)).astype(BF16)

    def step(e, s):
        first, last = RUNS[e]
        for u in range(first + 1, last - 1):
            descend(s, u)
        for _, side, u, to in ends[e]:
            here = halo.at[s, e, side]
            pltpu.make_async_copy(here, here, halo_recv.at[s, e, side]).wait()
            at_end = jnp.where(side == 0, tile[first] == 0, tile[last - 1] == ns * TL - 1)
            slot = jnp.where(side == 0, lslot[first], 3 - lslot[last - 1])
            away = jnp.where(at_end, rounded[s, u], halo[s, e, side])
            cone_acc[u] += dot(away, pats[slot])
            descend(s, u)
            if s < STEPS - 1:
                start_halo(s + 1, e, u, side, to)
        if s < STEPS - 1:
            cone_own(e, s + 1)
        if s == 1:
            for u in range(first, last):
                cen = average(2, u)
                up = f[u] - cen
                lin[u] = lin[u] + gain[u] + up - cen
                gain[u] = up

    def pack_back(k, e, values):
        v = jnp.concatenate([round16(values(u)).astype(F32) for u in range(*RUNS[e])], axis=0)
        v = round16(sum(dot_0(order_e if e else order[...], term) for term in split(v)))
        snd = bufs[k][e][0]
        if e:
            for i in range(nc):
                snd[i] = fold(v[8 * i:8 * i + 8]).astype(I16)
        else:
            snd[...] = v.astype(I16).reshape(nc, ROWS, TILE)
        send_back(k, e)

    def give_back(e):
        pack_back(2, e, lambda u: (f[u] - 0.5) * FRAC_CODE)
        for u in range(*RUNS[e]):
            gain[u] += f[u] - average(4, u)
        pack_back(3, e, lambda u: gain[u] * GAIN_CODE)

    first_center(1)
    take_linear(1)
    step(1, 0)
    take_fraction(0)
    first_center(0)
    step(1, 1)
    take_linear(0)
    step(0, 0)
    step(1, 2)
    step(0, 1)
    step(1, 3)
    give_back(1)
    step(0, 2)
    step(0, 3)
    give_back(0)

    def home(k, e, write):
        wait_all(k, e, a_recv, bufs[k][e][1])
        rcv = bufs[k][e][1]
        n = nc * ROWS
        if e:
            v = jnp.concatenate([unfold(wide(rcv[j])) for j in range(nc)], axis=0)
            mat = back[:, n:]
        else:
            v = wide(rcv[...].reshape(n, TILE))
            mat = back[:, :n]
        m = sum(dot(mat, term) for term in split(v))
        for t in range(TL):
            write(slice(t * TILE, (t + 1) * TILE), m[t * HOME:(t + 1) * HOME])

    def write_f(ln, m):
        out_f[:, ln] = m * (1.0 / FRAC_CODE) + 0.5

    def write_d(ln, m):
        out_d[:, ln] = dual_v[:, ln] + m * (1.0 / GAIN_CODE)

    def add_f(ln, m):
        out_f[:, ln] += m * (1.0 / FRAC_CODE)

    def add_d(ln, m):
        out_d[:, ln] += m * (1.0 / GAIN_CODE)

    home(2, 1, write_f)
    home(3, 1, write_d)
    home(2, 0, add_f)
    home(3, 0, add_d)
    for k in range(4):
        for e in range(2):
            wait_all(k, e, a_send, bufs[k][e][0])
    for s in range(STEPS):
        for e in range(2):
            for side in range(2):
                part = halo.at[s, e, side]
                pltpu.make_async_copy(part, part, halo_send.at[s, e, side]).wait()


def store(f, d, f_out, d_out, sem):
    copies = []
    for k in range(4):
        rows = pl.ds(k * PER, PER)
        copies.append(pltpu.make_async_copy(f.at[rows], f_out.at[rows], sem.at[2 * k]))
        copies.append(pltpu.make_async_copy(d.at[rows], d_out.at[rows], sem.at[2 * k + 1]))
    for c in copies:
        c.start()
    for c in copies:
        c.wait()


def body(start_fraction, ore_value, dual_price, patterns, cone_list, node_list, probability):
    ns, nc = lax.axis_size("space"), lax.axis_size("scen")
    blocks = start_fraction.shape[2]
    flat = (HOME, blocks)
    hbm = pl.BlockSpec(memory_space=pltpu.HBM)
    dma = pltpu.SemaphoreType.DMA
    v = pltpu.VMEM
    f, d = pl.pallas_call(
        functools.partial(kernel, ns, nc),
        out_shape=[v(flat, F32)] * 2,
        in_specs=[hbm] * 7,
        out_specs=[pl.BlockSpec(memory_space=v)] * 2,
        scratch_shapes=[
            pltpu.SMEM((2, TL, 3), jnp.int32),
            v((2, SCEN), jnp.int32),
            v((1, SCEN), F32),
            v(flat, BF16),
            v(flat, BF16),
            v(flat, F32),
            v((3, TILE, TILE), BF16),
            v((TL * HOME, TL * HOME), BF16),
            v((TL * HOME, TL * HOME), BF16),
            v((SCEN * MAIN, SCEN * MAIN), BF16),
            v((2, SCEN, SCEN), BF16),
            v((STEPS + 1, UNITS + 1, SCEN, TILE), BF16),
            v((STEPS, 2, 2, SCEN, TILE), BF16),
            v((UNITS, SCEN, TILE), F32),
            v((UNITS, SCEN, TILE), BF16),
            v((UNITS, SCEN, TILE), F32),
            v((UNITS, SCEN, TILE), F32),
            v((UNITS, SCEN, TILE), F32),
            *[v((nc, ROWS, TILE), kind) for kind in (BF16, BF16, *[I16] * 6)],
            *[v((nc, ROWS, HALF), kind) for kind in (BF16, BF16, *[I16] * 6)],
            v((2, TL, 3), jnp.int32),
            dma((7,)),
            dma((STEPS, 2, 2)),
            dma((STEPS, 2, 2)),
            dma((8,)),
            dma((8,)),
            dma((4,)),
        ],
        compiler_params=pltpu.CompilerParams(
            collective_id=0, has_side_effects=True, vmem_limit_bytes=56 * 2**20
        ),
    )(
        cone_list,
        node_list,
        probability.reshape(1, -1),
        start_fraction.reshape(flat),
        ore_value.reshape(flat),
        dual_price.reshape(flat),
        patterns,
    )
    f, d = pl.pallas_call(
        store,
        out_shape=[jax.ShapeDtypeStruct(flat, F32)] * 2,
        in_specs=[pl.BlockSpec(memory_space=pl.ANY)] * 2,
        out_specs=[hbm] * 2,
        scratch_shapes=[dma((8,))],
        compiler_params=pltpu.CompilerParams(vmem_limit_bytes=4 * 2**20),
    )(f, d)
    return f.reshape(start_fraction.shape), d.reshape(start_fraction.shape)


def solution(mesh):
    in_specs = (
        P("scen", None, "space"),
        P("scen", None, "space"),
        P("scen", None, "space"),
        P(),
        P("space", None),
        P(),
        P(),
    )
    out_specs = (P("scen", None, "space"), P("scen", None, "space"))
    return jax.shard_map(body, mesh=mesh, in_specs=in_specs, out_specs=out_specs, check_vma=False)
```
